32 devices in a mesh: sec: 4 (over y, x), dev: 8 (over z, core).
Axes of the slice: x: 2, y: 2, z: 4, core: 2. Of those that a mesh axis runs over, the one named last changes fastest.
Arguments:
- hidden: bfloat16 [512, 3584], P(('sec', 'dev')), may hold values from -6 to 6
- expert_ids: int32 [512, 8], P(('sec', 'dev')), may hold values from 0 to 31, all different within a row; in each aligned block of 16 rows (0 to 15, 16 to 31, ...) at most 8 rows name the same one
- route_weights: float32 [512, 8], P(('sec', 'dev')), may hold values from 0.1 to 1
- w_gate_up: bfloat16 [32, 3584, 2048], P(('sec', 'dev')), may hold values from -0.09375 to 0.09375
- w_down: bfloat16 [32, 1024, 3584], P(('sec', 'dev')), may hold values from -0.1875 to 0.1875
- query_latent: bfloat16 [128, 128, 512], P(('sec', 'dev')), may hold values from -400 to 400
- query_rope: bfloat16 [128, 64, 128], P(('sec', 'dev')), may hold values from -6 to 6
- latent_cache: bfloat16 [128, 512, 512], P(('sec', 'dev')), may hold values from -4 to 4
- rope_cache: bfloat16 [128, 64, 512], P(('sec', 'dev')), may hold values from -6 to 6
- cache_lengths: int32 [128], P(('sec', 'dev')), may hold values from 64 to 512
Outputs:
- moe_out: bfloat16 [512, 3584], P(('sec', 'dev'))
- expert_load: float32 [32], replicated
- attention_out: bfloat16 [128, 128, 512], P(('sec', 'dev'))
The draws below stay inside these ranges and needn't reach their ends.
Inputs may be any that keep to these rules, and one draw needn't show every extreme that they name: `expert_ids`: in the rows of one device no expert is named more than 8 times; in some device's rows some expert is named exactly 8 times.
All inputs are finite; a program needn't handle non-finite values.
Results may differ from the reference program's by a relative error of at most 0.008.
Values may be sent and summed in bfloat16 or wider, within the bound.
A program may use at most 128 MiB of HBM per device.

```python
import math
import jax
import jax.numpy as jnp
import numpy as np
from jax import lax

D = 3584
FF = 1024
TOPK = 8
HEADS = 128
LATENT = 512
ROPE = 64
LEN = 512
ROWS_DEV = 16
EXPERTS = 32
CAP = 8
TOKENS = 512
ATT_TOTAL = 128


def attention_pair(key):
    cache_key = jax.random.fold_in(key, 11)
    query_key = jax.random.fold_in(key, 12)
    latent = jnp.clip(jax.random.normal(cache_key, (ATT_TOTAL, LEN, LATENT), jnp.float32), -4.0, 4.0)
    queries = jnp.clip(jax.random.normal(query_key, (ATT_TOTAL, HEADS, LATENT), jnp.float32), -4.0, 4.0)
    return (latent, queries)


def draw_latent_cache(key, part):
    return attention_pair(key)[0].astype(jnp.bfloat16)


def draw_query_latent(key, part):
    return attention_pair(key)[1].astype(jnp.bfloat16)


def draw_cache_lengths(key, part):
    length_key = jax.random.fold_in(key, 21)
    lengths = jax.random.randint(length_key, (ATT_TOTAL,), max(6, LEN // 8), LEN + 1, dtype=jnp.int32)
    return lengths.at[0].set(LEN)


def steps_of(own_key, shape, pieces, least, high):
    factor_of, own = 1.0, jax.random.fold_in(own_key, 6)
    for dim, parts in pieces:
        draws = jnp.exp(jax.random.uniform(jax.random.fold_in(own, dim), (parts,), jnp.float32, least / len(pieces), high / len(pieces)))
        factor_of = factor_of * jnp.repeat(draws, shape[dim] // parts).reshape([-1 if axis == dim else 1 for axis in range(len(shape))])
    return factor_of


def shared_out(stream_key, own, number, rows, count, top, bound, lean):
    ranking = jax.random.permutation(stream_key, count)
    packed, ordinary = shares(count, rows * top, bound, lean, True), shares(count, rows * top, bound, lean, False)
    places = jnp.arange(count)

    def named(sizes, rotation):
        used = int((sizes > 0).sum())
        fixed = max(1, used // 4)
        moved = fixed + (places - fixed + rotation * (used - fixed)) % max(1, count - fixed)
        return jnp.zeros((count,), jnp.int32).at[ranking[jnp.where(places < fixed, places, moved)]].set(jnp.asarray(sizes, jnp.int32))

    sizes = jnp.where(number % 4 == 0, named(packed, number // 4), named(ordinary, number - number // 4 - 1))
    mixed = jax.random.permutation(jax.random.fold_in(own, 3), count)
    giver, taker = mixed[0:count // 2 * 2:2], mixed[1:count // 2 * 2:2]
    slack = jnp.minimum(sizes[giver] - 1, bound - sizes[taker]) // 2
    slack = jnp.where((giver == ranking[0]) | (taker == ranking[0]) | (sizes[taker] == 0), 0, jnp.maximum(slack, 0))
    moved = jax.random.randint(jax.random.fold_in(own, 4), (count // 2,), 0, 1 << 20) % (slack + 1)
    sizes = sizes.at[giver].add(-moved).at[taker].add(moved)
    items = jnp.searchsorted(jnp.cumsum(sizes), jnp.arange(rows * top), side="right").astype(jnp.int32)
    grid = items.reshape(top, rows).T
    grid = grid[jax.random.permutation(jax.random.fold_in(own, 1), rows)]
    rotation = jax.random.randint(jax.random.fold_in(own, 2), (rows, 1), 0, top)
    return jnp.take_along_axis(grid, (jnp.arange(top)[None, :] + rotation) % top, axis=1)


def shares(number_of, total, limit, lean, full):
    loads = [(1 << 20) // math.isqrt(grade ** lean) + 1 for grade in range(1, number_of + 1)]
    largest = limit if full else min(limit, max(-(-total // number_of), total * loads[0] // sum(loads)))
    least = 1 if total - largest >= number_of - 1 else 0
    holding, rest = [largest] + [least] * (number_of - 1), total - largest - least * (number_of - 1)
    while rest > 0:
        movable = [i for i in range(1, number_of) if holding[i] < largest] or [i for i in range(1, number_of) if holding[i] < limit]
        pool, remaining = sum([loads[i] for i in movable]), rest
        for i in movable:
            extra = min(limit - holding[i], max(1, remaining * loads[i] // pool), rest)
            holding[i] = holding[i] + extra
            rest = rest - extra
    return np.array(holding)


def gaussian(own_key, shape, scale, limit, shards=(), kind=jnp.bfloat16):
    values = jax.random.normal(own_key, shape, jnp.float32) * scale
    if len(shards) > 0:
        values = steps_of(own_key, shape, shards, -0.22, 0.18) * values
    return jnp.clip(values, min=-limit, max=limit).astype(kind)


def setup_inputs(seed: int = 0) -> dict:
    seeds = jax.random.split(jax.random.key(seed), 11)
    hidden = gaussian(seeds[0], (TOKENS, D), 1.0, 6.0, ((0, 32),))
    expert_ids_keys = jax.random.split(jax.random.fold_in(seeds[1], 1), TOKENS // ROWS_DEV)
    expert_ids_turns = jax.random.permutation(jax.random.fold_in(seeds[1], 3), TOKENS // ROWS_DEV)
    expert_ids = jax.vmap(lambda own, number: shared_out(jax.random.fold_in(seeds[1], 2), own, number, ROWS_DEV, EXPERTS, TOPK, CAP, 2))(expert_ids_keys, expert_ids_turns).reshape((TOKENS, TOPK))
    route_weights = jnp.clip(0.1 + 0.9 * jax.random.uniform(seeds[2], (TOKENS, TOPK), jnp.float32) ** steps_of(seeds[2], (TOKENS, TOPK), ((0, 32),), -0.2, 0.2), 0.1, 1.0)
    w_gate_up = gaussian(seeds[3], (EXPERTS, D, 2 * FF), D ** -0.5, 0.09375, ((0, 32),))
    w_down = gaussian(seeds[4], (EXPERTS, FF, D), FF ** -0.5, 0.1875, ((0, 32),))
    query_latent = draw_query_latent(jax.random.fold_in(seeds[10], 71), 0)
    query_rope = gaussian(seeds[6], (ATT_TOTAL, ROPE, HEADS), 1.0, 6.0, ((0, 32),))
    latent_cache = draw_latent_cache(jax.random.fold_in(seeds[10], 71), 0)
    rope_cache = gaussian(seeds[8], (ATT_TOTAL, ROPE, LEN), 1.0, 6.0, ((0, 32),))
    cache_lengths = draw_cache_lengths(jax.random.fold_in(seeds[10], 71), 0)
    return {"hidden": hidden, "expert_ids": expert_ids, "route_weights": route_weights, "w_gate_up": w_gate_up, "w_down": w_down, "query_latent": query_latent, "query_rope": query_rope, "latent_cache": latent_cache, "rope_cache": rope_cache, "cache_lengths": cache_lengths}


def attend(query_latent, query_rope, latent_cache, rope_cache, cache_lengths):
    factor = (query_latent.shape[2] + query_rope.shape[1]) ** -0.5
    scores = jnp.einsum("rhc,rtc->rht", query_latent.astype(jnp.float32), latent_cache.astype(jnp.float32))
    scores = scores + jnp.einsum("rph,rpt->rht", query_rope.astype(jnp.float32), rope_cache.astype(jnp.float32))
    scores = scores * factor
    positions = jnp.arange(latent_cache.shape[1], dtype=jnp.int32)
    live_mask = positions[None, None, :] < cache_lengths.astype(jnp.int32)[:, None, None]
    scores = jnp.where(live_mask, scores, -1e30)
    highest = jnp.max(scores, axis=-1, keepdims=True)
    powers = jnp.exp(scores - highest)
    attention_weights = (powers / jnp.sum(powers, axis=-1, keepdims=True)).astype(jnp.bfloat16)
    result = jnp.einsum("rht,rtc->rhc", attention_weights.astype(jnp.float32), latent_cache.astype(jnp.float32))
    return result.astype(jnp.bfloat16)


def reference(hidden, expert_ids, route_weights, w_gate_up, w_down, query_latent, query_rope, latent_cache, rope_cache, cache_lengths):
    token_count, model_width = hidden.shape
    experts = w_gate_up.shape[0]
    hidden_units = w_down.shape[1]
    blocks = token_count // ROWS_DEV
    grouped = expert_ids.reshape(blocks, ROWS_DEV * TOPK).astype(jnp.int32)
    onehot = (grouped[:, :, None] == jnp.arange(experts, dtype=jnp.int32)[None, None, :]).astype(jnp.int32)
    earlier = jnp.cumsum(onehot, axis=1) - onehot
    rank_in = jnp.sum(earlier * onehot, axis=2)
    position = (jnp.arange(blocks, dtype=jnp.int32)[:, None] * CAP + rank_in).reshape(-1).astype(jnp.int32)
    flat_ids = expert_ids.reshape(-1).astype(jnp.int32)
    row_index = (jnp.arange(token_count * TOPK, dtype=jnp.int32) // TOPK).astype(jnp.int32)
    slot_table = jnp.zeros((experts, blocks * CAP), jnp.int32).at[flat_ids, position].set(row_index)
    weight_table = jnp.zeros((experts, blocks * CAP), jnp.float32).at[flat_ids, position].set(route_weights.reshape(-1))

    def one_expert(accumulated, expert):
        chosen_rows = slot_table[expert]
        inputs = hidden[chosen_rows]
        projected = jnp.dot(inputs, w_gate_up[expert], preferred_element_type=jnp.float32)
        activated = (jax.nn.silu(projected[:, :hidden_units]) * projected[:, hidden_units:]).astype(jnp.bfloat16)
        produced = jnp.dot(activated, w_down[expert], preferred_element_type=jnp.float32).astype(jnp.bfloat16)
        accumulated = accumulated.at[chosen_rows].add(weight_table[expert][:, None] * produced.astype(jnp.float32))
        return accumulated, None

    accumulated, unused = lax.scan(one_expert, jnp.zeros((token_count, model_width), jnp.float32), jnp.arange(experts, dtype=jnp.int32))
    moe_out = accumulated.astype(jnp.bfloat16)
    counts = jnp.sum(onehot, axis=(0, 1)).astype(jnp.float32)
    expert_load = counts / (token_count * TOPK / experts)
    attention_out = attend(query_latent, query_rope, latent_cache, rope_cache, cache_lengths)
    return (moe_out, expert_load, attention_out)
```

```python
import jax
import jax.numpy as jnp
from jax import lax
from jax.sharding import PartitionSpec as P


def attend(query_latent, query_rope, latent_cache, rope_cache, cache_lengths):
    factor = (query_latent.shape[2] + query_rope.shape[1]) ** (-0.5)
    scores = jnp.einsum(
        "rhc,rtc->rht", query_latent, latent_cache, preferred_element_type=jnp.float32
    )
    scores = scores + jnp.einsum(
        "rph,rpt->rht", query_rope, rope_cache, preferred_element_type=jnp.float32
    )
    scores = scores * factor
    positions = jnp.arange(latent_cache.shape[1], dtype=jnp.int32)
    live_mask = positions[None, None, :] < cache_lengths[:, None, None]
    scores = jnp.where(live_mask, scores, -1e30)
    highest = jnp.max(scores, axis=-1, keepdims=True)
    powers = jnp.exp(scores - highest)
    attention_weights = (powers / jnp.sum(powers, axis=-1, keepdims=True)).astype(jnp.bfloat16)
    result = jnp.einsum(
        "rht,rtc->rhc", attention_weights, latent_cache, preferred_element_type=jnp.float32
    )
    return result.astype(jnp.bfloat16)


def per_device(
    hidden,
    expert_ids,
    route_weights,
    w_gate_up,
    w_down,
    query_latent,
    query_rope,
    latent_cache,
    rope_cache,
    cache_lengths,
):
    axes = ("sec", "dev")
    row_count, model_width = hidden.shape
    top_count = expert_ids.shape[1]
    experts = lax.axis_size("sec") * lax.axis_size("dev")
    capacity = 2 * row_count * top_count // experts
    me = lax.axis_index("sec") * lax.axis_size("dev") + lax.axis_index("dev")
    routes = jnp.concatenate([expert_ids.astype(jnp.float32), route_weights], axis=1)
    routes = lax.all_gather(routes, axes, axis=0, tiled=True)
    rows = lax.all_gather(hidden, axes, axis=0, tiled=True)
    all_ids = routes[:, :top_count].astype(jnp.int32)
    hit = all_ids == me
    weight = jnp.sum(jnp.where(hit, routes[:, top_count:], 0.0), axis=1)
    chosen = jnp.any(hit, axis=1).astype(jnp.int32).reshape(experts, row_count)
    rank = jnp.cumsum(chosen, axis=1) - chosen
    slot = jnp.where(chosen > 0, jnp.arange(experts)[:, None] * capacity + rank, -1).reshape(-1)
    placer = (jnp.arange(experts * capacity)[:, None] == slot[None, :]).astype(jnp.bfloat16)
    received = jnp.dot(placer, rows, preferred_element_type=jnp.float32).astype(jnp.bfloat16)
    projected = jnp.dot(received, w_gate_up[0], preferred_element_type=jnp.float32)
    hidden_units = w_down.shape[1]
    activated = (jax.nn.silu(projected[:, :hidden_units]) * projected[:, hidden_units:]).astype(
        jnp.bfloat16
    )
    produced = jnp.dot(activated, w_down[0], preferred_element_type=jnp.float32).astype(
        jnp.bfloat16
    )
    spread = lax.dot_general(
        placer, produced, (((0,), (0,)), ((), ())), preferred_element_type=jnp.float32
    )
    partial = (spread * weight[:, None]).astype(jnp.bfloat16)
    moe_out = lax.psum_scatter(partial, axes, scatter_dimension=0, tiled=True)
    expert_range = jnp.arange(experts, dtype=jnp.int32)
    counts = jnp.sum((all_ids.reshape(-1)[:, None] == expert_range).astype(jnp.float32), axis=0)
    expert_load = counts / float(row_count * top_count)
    attention_out = attend(query_latent, query_rope, latent_cache, rope_cache, cache_lengths)
    return (moe_out, expert_load, attention_out)


def solution(mesh):
    return jax.shard_map(
        per_device,
        mesh=mesh,
        in_specs=(
            P(("sec", "dev"), None),
            P(("sec", "dev"), None),
            P(("sec", "dev"), None),
            P(("sec", "dev"), None, None),
            P(("sec", "dev"), None, None),
            P(("sec", "dev"), None, None),
            P(("sec", "dev"), None, None),
            P(("sec", "dev"), None, None),
            P(("sec", "dev"), None, None),
            P(("sec", "dev")),
        ),
        out_specs=(P(("sec", "dev"), None), P(), P(("sec", "dev"), None, None)),
        check_vma=False,
    )
```

```python
import functools

import jax
import jax.numpy as jnp
from jax import lax
from jax.experimental import pallas as pl
from jax.experimental.pallas import tpu as pltpu
from jax.sharding import PartitionSpec as P

WIDTH = 512
MESH = pl.DeviceIdType.MESH
F32 = jnp.float32
BF16 = jnp.bfloat16


def kernel(
    slots_per,
    x_ref,
    table_ref,
    lengths_ref,
    gate_up_hbm,
    down_hbm,
    ql_hbm,
    qr_hbm,
    lat_hbm,
    rope_hbm,
    out_ref,
    load_ref,
    att_ref,
    rows_buf,
    table_buf,
    gate_up,
    down,
    ql,
    qr,
    lat,
    rope,
    projected,
    activated,
    placer,
    placer_t,
    weight,
    from_sib,
    from_first,
    from_second,
    from_line,
    local_sem,
    line_send,
    line_recv,
    hop_send,
    hop_recv,
    back_send,
    back_recv,
    back_line_send,
    back_line_recv,
):
    chunks = rows_buf.shape[0]
    line = rows_buf.shape[3]
    rows = x_ref.shape[0]
    tokens = 2 * 4 * line * rows
    units = down.shape[0]
    s = lax.axis_index("sec")
    d = lax.axis_index("dev")
    m = d // 2
    k = lax.rem(d, 2)
    experts = 8 * line
    me = s * (2 * line) + d

    def xor(j):
        low = lax.rem(s, 2)
        high = s // 2
        if j & 1:
            low = 1 - low
        if j & 2:
            high = 1 - high
        return high * 2 + low

    secs = [s, xor(1), xor(2), xor(3)]
    sib = (s, m * 2 + (1 - k))
    across = {1: (secs[1], d), 2: (secs[2], d)}

    def on_line(step):
        return (s, lax.rem(m + step, line) * 2 + k)

    local = []

    def fetch(src, dst):
        copy = pltpu.make_async_copy(src, dst, local_sem.at[len(local)])
        copy.start()
        local.append(copy)
        return copy

    partners = [sib, across[1], across[2]] + [on_line(i) for i in range(1, line)]
    barrier = pltpu.get_barrier_semaphore()
    for partner in partners:
        pl.semaphore_signal(barrier, inc=1, device_id=partner, device_id_type=MESH)
    att_copies = [fetch(a, b) for a, b in ((ql_hbm, ql), (qr_hbm, qr), (lat_hbm, lat), (rope_hbm, rope))]
    gate_copies = [
        fetch(gate_up_hbm.at[0, pl.ds(c * WIDTH, WIDTH)], gate_up.at[pl.ds(c * WIDTH, WIDTH)])
        for c in range(chunks)
    ]
    down_copy = fetch(down_hbm.at[0], down)

    table_buf[k, s, m] = table_ref[...]
    for c in range(chunks):
        rows_buf[c, k, s, m] = x_ref[:, c * WIDTH : (c + 1) * WIDTH]
    pl.semaphore_wait(barrier, len(partners))

    started = []

    def send(src, dst, send_sem, recv_sem, device):
        copy = pltpu.make_async_remote_copy(
            src_ref=src, dst_ref=dst, send_sem=send_sem, recv_sem=recv_sem,
            device_id=device, device_id_type=MESH,
        )
        copy.start()
        started.append(copy)
        return copy

    pieces = [table_buf] + [rows_buf.at[c] for c in range(chunks)]
    line_copies, own, fwd, sibs = {}, {}, {}, {}
    for i, buf in enumerate(pieces):
        line_copies[i] = [
            send(buf.at[k, s, m], buf.at[k, s, m], line_send.at[i, j - 1], line_recv.at[i, j - 1], on_line(j))
            for j in range(1, line)
        ]

    def hop(i, group, kind, device):
        buf = pieces[i]
        return send(buf.at[k, group], buf.at[k, group], hop_send.at[i, kind], hop_recv.at[i, kind], device)

    def stage_own(i):
        for copy in line_copies[i]:
            copy.wait_recv()
        own[i] = [hop(i, s, 0, across[1]), hop(i, s, 1, across[2])]
        sibs[i] = [hop(i, s, 3, sib)]

    def stage_cross(i):
        own[i][i % 2].wait_recv()
        fwd[i] = hop(i, secs[1 + i % 2], 2, across[2 - i % 2])
        sibs[i].append(hop(i, secs[1 + i % 2], 4, sib))
        own[i][1 - i % 2].wait_recv()
        sibs[i].append(hop(i, secs[2 - i % 2], 5, sib))

    def stage_diagonal(i):
        fwd[i].wait_recv()
        sibs[i].append(hop(i, secs[3], 6, sib))

    def routing():
        lanes = table_buf.shape[-1]
        part = 8 * rows
        table = table_buf[...].reshape(tokens, lanes)
        chosen = (table > 0.0).astype(F32)
        load_ref[...] = jnp.sum(chosen, axis=0, keepdims=True) / float(tokens * slots_per[1] // experts)
        lane = lax.broadcasted_iota(jnp.int32, (tokens, lanes), 1)
        mine = jnp.sum(jnp.where(lane == me, table, 0.0), axis=1, keepdims=True)
        weight[...] = mine
        r = lax.broadcasted_iota(jnp.int32, (part, part), 0)
        q = lax.broadcasted_iota(jnp.int32, (part, part), 1)
        before = jnp.where((r // rows == q // rows) & (q < r), 1.0, 0.0).astype(BF16)
        for b in range(tokens // part):
            cut = slice(b * part, (b + 1) * part)
            hit = (mine[cut] > 0.0).astype(F32)
            rank = jnp.dot(before, jnp.broadcast_to(hit, (part, 128)).astype(BF16), preferred_element_type=F32)[:, :1]
            block = lax.broadcasted_iota(jnp.int32, (part, 1), 0) // rows + b * 8
            slot = jnp.where(hit > 0.0, block.astype(F32) * float(slots_per[0]) + rank, -1.0)
            spots = lax.broadcasted_iota(jnp.int32, (part, experts * slots_per[0]), 1).astype(F32)
            picks = jnp.where(spots == slot, 1.0, 0.0)
            placer_t[cut, :] = picks.astype(BF16)
            placer[:, cut] = picks.T.astype(BF16)

    def attend(r):
        scores = lax.dot_general(ql[r], lat[r], (((1,), (1,)), ((), ())), preferred_element_type=F32)
        scores = scores + lax.dot_general(qr[r], rope[r], (((0,), (0,)), ((), ())), preferred_element_type=F32)
        scores = scores * ((ql.shape[2] + qr.shape[1]) ** -0.5)
        positions = lax.broadcasted_iota(jnp.int32, scores.shape, 1)
        scores = jnp.where(positions < lengths_ref[r], scores, -1e30)
        powers = jnp.exp(scores - jnp.max(scores, axis=-1, keepdims=True))
        weights = (powers / jnp.sum(powers, axis=-1, keepdims=True)).astype(BF16)
        att_ref[r] = jnp.dot(weights, lat[r], preferred_element_type=F32).astype(BF16)

    def stage_up(i):
        for copy in sibs[i]:
            copy.wait_recv()
        if i == 0:
            routing()
            return
        c = i - 1
        gate_copies[c].wait()
        received = jnp.dot(
            placer[...], rows_buf[c].reshape(tokens, WIDTH), preferred_element_type=F32
        ).astype(BF16)

        @pl.loop(0, 2 * units // 512)
        def _(t):
            cols = pl.ds(pl.multiple_of(t * 512, 512), 512)
            part = jnp.dot(received, gate_up[pl.ds(c * WIDTH, WIDTH), cols], preferred_element_type=F32)
            if c == 0:
                projected[:, cols] = part
            else:
                projected[:, cols] += part

    count = chunks + 1
    for copy in att_copies:
        copy.wait()
    att_rows = ql.shape[0]
    attended = 0
    for i in range(count + 3):
        if i < count:
            stage_own(i)
        if 0 <= i - 1 < count:
            stage_cross(i - 1)
        if 0 <= i - 2 < count:
            stage_diagonal(i - 2)
        if attended < att_rows:
            attend(attended)
            attended += 1
        if 0 <= i - 3 < count:
            stage_up(i - 3)
    for r in range(attended, att_rows):
        attend(r)
    for copy in started:
        copy.wait_send()

    for t in range(0, units, 256):
        gate = projected[:, t : t + 256]
        up = projected[:, units + t : units + t + 256]
        activated[:, t : t + 256] = (gate / (1.0 + jnp.exp(-gate)) * up).astype(BF16)
    down_copy.wait()

    started.clear()
    sib_in, first_in, second_in, line_in = {}, {}, {}, {}

    def stage_down(c):
        produced = jnp.dot(
            activated[...], down[:, c * WIDTH : (c + 1) * WIDTH], preferred_element_type=F32
        ).astype(BF16)
        half = tokens // 2
        for side in (0, 1):
            group = (1 - k) if side == 0 else k
            start = pl.multiple_of(group * half, half)
            spread = jnp.dot(placer_t[pl.ds(start, half), :], produced, preferred_element_type=F32)
            spread = spread * weight[pl.ds(start, half), :]
            rows_buf[c, group] = spread.astype(BF16).reshape(4, line, rows, WIDTH)
            if side == 0:
                sib_in[c] = send(rows_buf.at[c, group], from_sib.at[c], back_send.at[c, 0], back_recv.at[c, 0], sib)

    def add(c, group, value):
        rows_buf[c, k, group] = (rows_buf[c, k, group].astype(F32) + value.astype(F32)).astype(BF16)

    def stage_first(c):
        sib_in[c].wait_recv()
        one = 1 + c % 2
        for j in (one, 3, 3 - one, 0):
            add(c, secs[j], from_sib[c, secs[j]])
            if j == one:
                a = send(rows_buf.at[c, k, secs[one]], from_first.at[c, 0], back_send.at[c, 1], back_recv.at[c, 1], across[one])
            if j == 3:
                b = send(rows_buf.at[c, k, secs[3]], from_first.at[c, 1], back_send.at[c, 2], back_recv.at[c, 2], across[one])
        first_in[c] = [a, b]

    def stage_second(c):
        two = 2 - c % 2
        for copy in first_in[c]:
            copy.wait_recv()
        add(c, secs[two], from_first[c, 1])
        second_in[c] = send(rows_buf.at[c, k, secs[two]], from_second.at[c], back_send.at[c, 3], back_recv.at[c, 3], across[two])
        add(c, s, from_first[c, 0])

    def stage_line(c):
        second_in[c].wait_recv()
        add(c, s, from_second[c])
        line_in[c] = [
            send(
                rows_buf.at[c, k, s, lax.rem(m + j, line)], from_line.at[c, j - 1],
                back_line_send.at[c, j - 1], back_line_recv.at[c, j - 1], on_line(j),
            )
            for j in range(1, line)
        ]

    def stage_out(c):
        total = rows_buf[c, k, s, m].astype(F32)
        for j, copy in enumerate(line_in[c]):
            copy.wait_recv()
            total = total + from_line[c, j].astype(F32)
        out_ref[:, c * WIDTH : (c + 1) * WIDTH] = total.astype(BF16)

    for i in range(chunks + 4):
        for lag, stage in enumerate((stage_down, stage_first, stage_second, stage_line, stage_out)):
            if 0 <= i - lag < chunks:
                stage(i - lag)
    for copy in started:
        copy.wait_send()


def per_device(
    hidden,
    expert_ids,
    route_weights,
    w_gate_up,
    w_down,
    query_latent,
    query_rope,
    latent_cache,
    rope_cache,
    cache_lengths,
):
    rows, model_width = hidden.shape
    top_count = expert_ids.shape[1]
    members = lax.axis_size("dev")
    experts = lax.axis_size("sec") * members
    line = members // 2
    capacity = 2 * rows * top_count // experts
    slots = experts * capacity
    tokens = experts * rows
    units = w_down.shape[1]
    lanes = -(-experts // 128) * 128
    chunks = model_width // WIDTH
    pieces = chunks + 1
    att_rows = query_latent.shape[0]
    hits = expert_ids[:, :, None] == jnp.arange(lanes, dtype=jnp.int32)
    table = jnp.sum(jnp.where(hits, route_weights[:, :, None], 0.0), axis=1)
    vmem = pl.BlockSpec(memory_space=pltpu.VMEM)
    smem = pl.BlockSpec(memory_space=pltpu.SMEM)
    hbm = pl.BlockSpec(memory_space=pl.ANY)
    dma = pltpu.SemaphoreType.DMA
    moe_out, load, attention_out = pl.pallas_call(
        functools.partial(kernel, (capacity, top_count)),
        out_shape=(
            jax.ShapeDtypeStruct((rows, model_width), BF16),
            jax.ShapeDtypeStruct((1, lanes), F32),
            jax.ShapeDtypeStruct(query_latent.shape, BF16),
        ),
        in_specs=[vmem, vmem, smem, hbm, hbm, hbm, hbm, hbm, hbm],
        out_specs=(vmem, vmem, vmem),
        scratch_shapes=[
            pltpu.VMEM((chunks, 2, 4, line, rows, WIDTH), BF16),
            pltpu.VMEM((2, 4, line, rows, lanes), F32),
            pltpu.VMEM(w_gate_up.shape[1:], BF16),
            pltpu.VMEM(w_down.shape[1:], BF16),
            pltpu.VMEM(query_latent.shape, BF16),
            pltpu.VMEM(query_rope.shape, BF16),
            pltpu.VMEM(latent_cache.shape, BF16),
            pltpu.VMEM(rope_cache.shape, BF16),
            pltpu.VMEM((slots, 2 * units), F32),
            pltpu.VMEM((slots, units), BF16),
            pltpu.VMEM((slots, tokens), BF16),
            pltpu.VMEM((tokens, slots), BF16),
            pltpu.VMEM((tokens, 1), F32),
            pltpu.VMEM((chunks, 4, line, rows, WIDTH), BF16),
            pltpu.VMEM((chunks, 2, line, rows, WIDTH), BF16),
            pltpu.VMEM((chunks, line, rows, WIDTH), BF16),
            pltpu.VMEM((chunks, line - 1, rows, WIDTH), BF16),
            dma((chunks + 5,)),
            dma((pieces, line - 1)),
            dma((pieces, line - 1)),
            dma((pieces, 7)),
            dma((pieces, 7)),
            dma((chunks, 4)),
            dma((chunks, 4)),
            dma((chunks, line - 1)),
            dma((chunks, line - 1)),
        ],
        compiler_params=pltpu.CompilerParams(
            collective_id=0, has_side_effects=True, vmem_limit_bytes=62 * 1024 * 1024
        ),
        name="experts_and_attention",
    )(
        hidden, table, cache_lengths, w_gate_up, w_down,
        query_latent, query_rope, latent_cache, rope_cache,
    )
    return (moe_out, load[0, :experts], attention_out)


def solution(mesh):
    return jax.shard_map(
        per_device,
        mesh=mesh,
        in_specs=(
            P(("sec", "dev"), None),
            P(("sec", "dev"), None),
            P(("sec", "dev"), None),
            P(("sec", "dev"), None, None),
            P(("sec", "dev"), None, None),
            P(("sec", "dev"), None, None),
            P(("sec", "dev"), None, None),
            P(("sec", "dev"), None, None),
            P(("sec", "dev"), None, None),
            P(("sec", "dev")),
        ),
        out_specs=(P(("sec", "dev"), None), P(), P(("sec", "dev"), None, None)),
        check_vma=False,
    )
```

```python
import functools

import jax
import jax.numpy as jnp
from jax import lax
from jax.experimental import pallas as pl
from jax.experimental.pallas import tpu as pltpu
from jax.sharding import PartitionSpec as P

WIDTH = 256
MESH = pl.DeviceIdType.MESH
F32 = jnp.float32
BF16 = jnp.bfloat16


def kernel(
    slots_per,
    x_ref,
    ids_ref,
    route_ref,
    lengths_ref,
    gate_up_hbm,
    down_hbm,
    ql_hbm,
    qr_hbm,
    lat_hbm,
    rope_hbm,
    out_ref,
    load_ref,
    att_ref,
    rows_buf,
    table_buf,
    gate_up,
    down,
    ql,
    qr,
    lat,
    rope,
    projected,
    activated,
    placer,
    placer_t,
    weight,
    from_sib,
    from_first,
    from_second,
    from_line,
    local_sem,
    line_send,
    line_recv,
    hop_send,
    hop_recv,
    back_send,
    back_recv,
    back_line_send,
    back_line_recv,
):
    chunks = rows_buf.shape[0]
    line = rows_buf.shape[3]
    rows = x_ref.shape[0]
    tokens = 2 * 4 * line * rows
    units = down.shape[0]
    s = lax.axis_index("sec")
    d = lax.axis_index("dev")
    m = d // 2
    k = lax.rem(d, 2)
    experts = 8 * line
    me = s * (2 * line) + d

    def xor(j):
        low = lax.rem(s, 2)
        high = s // 2
        if j & 1:
            low = 1 - low
        if j & 2:
            high = 1 - high
        return high * 2 + low

    secs = [s, xor(1), xor(2), xor(3)]
    sib = (s, m * 2 + (1 - k))
    across = {1: (secs[1], d), 2: (secs[2], d)}

    def on_line(step):
        return (s, lax.rem(m + step, line) * 2 + k)

    local = []

    def fetch(src, dst):
        copy = pltpu.make_async_copy(src, dst, local_sem.at[len(local)])
        copy.start()
        local.append(copy)
        return copy

    partners = [sib, across[1], across[2]] + [on_line(i) for i in range(1, line)]
    barrier = pltpu.get_barrier_semaphore()
    for partner in partners:
        pl.semaphore_signal(barrier, inc=1, device_id=partner, device_id_type=MESH)
    att_copies = [fetch(a, b) for a, b in ((ql_hbm, ql), (qr_hbm, qr), (lat_hbm, lat), (rope_hbm, rope))]
    gate_copies = []

    def fetch_gate():
        cut = pl.ds(len(gate_copies) * WIDTH, WIDTH)
        gate_copies.append(fetch(gate_up_hbm.at[0, cut], gate_up.at[cut]))

    for _ in range(2):
        fetch_gate()
    lanes = table_buf.shape[-1]
    names = lax.broadcasted_iota(jnp.int32, (lanes, rows), 0)
    table = jnp.zeros((lanes, rows), F32)
    for j in range(ids_ref.shape[0]):
        table = table + jnp.where(names == ids_ref[j : j + 1, :], route_ref[j : j + 1, :], 0.0)
    table_buf[k, s, m] = table.T
    for c in range(chunks):
        rows_buf[c, k, s, m] = x_ref[:, c * WIDTH : (c + 1) * WIDTH]
    pl.semaphore_wait(barrier, len(partners))

    started = []

    def send(src, dst, send_sem, recv_sem, device):
        copy = pltpu.make_async_remote_copy(
            src_ref=src, dst_ref=dst, send_sem=send_sem, recv_sem=recv_sem,
            device_id=device, device_id_type=MESH,
        )
        copy.start()
        started.append(copy)
        return copy

    pieces = [table_buf] + [rows_buf.at[c] for c in range(chunks)]
    line_copies, own, fwd, sibs = {}, {}, {}, {}
    for i, buf in enumerate(pieces):
        line_copies[i] = [
            send(buf.at[k, s, m], buf.at[k, s, m], line_send.at[i, j - 1], line_recv.at[i, j - 1], on_line(j))
            for j in range(1, line)
        ]

    def hop(i, group, kind, device):
        buf = pieces[i]
        return send(buf.at[k, group], buf.at[k, group], hop_send.at[i, kind], hop_recv.at[i, kind], device)

    def stage_own(i):
        for copy in line_copies[i]:
            copy.wait_recv()
        own[i] = [hop(i, s, 0, across[1]), hop(i, s, 1, across[2])]
        sibs[i] = [hop(i, s, 3, sib)]

    def stage_cross(i):
        own[i][i % 2].wait_recv()
        fwd[i] = hop(i, secs[1 + i % 2], 2, across[2 - i % 2])
        sibs[i].append(hop(i, secs[1 + i % 2], 4, sib))
        own[i][1 - i % 2].wait_recv()
        sibs[i].append(hop(i, secs[2 - i % 2], 5, sib))

    def stage_diagonal(i):
        fwd[i].wait_recv()
        sibs[i].append(hop(i, secs[3], 6, sib))

    def routing():
        part = 8 * rows
        table = table_buf[...].reshape(tokens, lanes)
        chosen = (table > 0.0).astype(F32)
        load = jnp.sum(chosen, axis=0, keepdims=True) / float(tokens * slots_per[1] // experts)
        load_ref[...] = load[:, :experts]
        lane = lax.broadcasted_iota(jnp.int32, (tokens, lanes), 1)
        mine = jnp.sum(jnp.where(lane == me, table, 0.0), axis=1, keepdims=True)
        weight[...] = mine
        r = lax.broadcasted_iota(jnp.int32, (part, part), 0)
        q = lax.broadcasted_iota(jnp.int32, (part, part), 1)
        before = jnp.where((r // rows == q // rows) & (q < r), 1.0, 0.0).astype(BF16)
        for b in range(tokens // part):
            cut = slice(b * part, (b + 1) * part)
            hit = (mine[cut] > 0.0).astype(F32)
            rank = jnp.dot(before, jnp.broadcast_to(hit, (part, 128)).astype(BF16), preferred_element_type=F32)[:, :1]
            block = lax.broadcasted_iota(jnp.int32, (part, 1), 0) // rows + b * 8
            slot = jnp.where(hit > 0.0, block.astype(F32) * float(slots_per[0]) + rank, -1.0)
            spots = lax.broadcasted_iota(jnp.int32, (part, experts * slots_per[0]), 1).astype(F32)
            picks = jnp.where(spots == slot, 1.0, 0.0)
            placer_t[cut, :] = picks.astype(BF16)
            placer[:, cut] = picks.T.astype(BF16)

    def attend(r):
        scores = lax.dot_general(ql[r], lat[r], (((1,), (1,)), ((), ())), preferred_element_type=F32)
        scores = scores + lax.dot_general(qr[r], rope[r], (((0,), (0,)), ((), ())), preferred_element_type=F32)
        scores = scores * ((ql.shape[2] + qr.shape[1]) ** -0.5)
        positions = lax.broadcasted_iota(jnp.int32, scores.shape, 1)
        scores = jnp.where(positions < lengths_ref[r], scores, -1e30)
        powers = jnp.exp(scores - jnp.max(scores, axis=-1, keepdims=True))
        weights = (powers / jnp.sum(powers, axis=-1, keepdims=True)).astype(BF16)
        att_ref[r] = jnp.dot(weights, lat[r], preferred_element_type=F32).astype(BF16)

    def stage_up(i):
        for copy in sibs[i]:
            copy.wait_recv()
        if i == 0:
            routing()
            return
        c = i - 1
        gate_copies[c].wait()
        received = jnp.dot(
            placer[...], rows_buf[c].reshape(tokens, WIDTH), preferred_element_type=F32
        ).astype(BF16)

        @pl.loop(0, 2 * units // 512)
        def _(t):
            cols = pl.ds(pl.multiple_of(t * 512, 512), 512)
            part = jnp.dot(received, gate_up[pl.ds(c * WIDTH, WIDTH), cols], preferred_element_type=F32)
            if c == 0:
                projected[:, cols] = part
            else:
                projected[:, cols] += part

    count = chunks + 1
    for copy in att_copies:
        copy.wait()
    att_rows = ql.shape[0]
    attended = 0
    for i in range(count + 5):
        if i < count:
            stage_own(i)
        if 0 <= i - 2 < count:
            stage_cross(i - 2)
        if 0 <= i - 4 < count:
            stage_diagonal(i - 4)
        if len(gate_copies) < chunks:
            fetch_gate()
        if i == 4:
            down_copy = fetch(down_hbm.at[0], down)
        if attended < att_rows and i >= 1:
            attend(attended)
            attended += 1
        if 0 <= i - 5 < count:
            stage_up(i - 5)
    for r in range(attended, att_rows):
        attend(r)
    for copy in started:
        copy.wait_send()

    for t in range(0, units, 256):
        gate = projected[:, t : t + 256]
        up = projected[:, units + t : units + t + 256]
        activated[:, t : t + 256] = (gate / (1.0 + jnp.exp(-gate)) * up).astype(BF16)
    down_copy.wait()

    started.clear()
    sib_in, first_in, second_in, line_in = {}, {}, {}, {}

    def stage_down(c):
        produced = jnp.dot(
            activated[...], down[:, c * WIDTH : (c + 1) * WIDTH], preferred_element_type=F32
        ).astype(BF16)
        half = tokens // 2
        for side in (0, 1):
            group = (1 - k) if side == 0 else k
            start = pl.multiple_of(group * half, half)
            spread = jnp.dot(placer_t[pl.ds(start, half), :], produced, preferred_element_type=F32)
            spread = spread * weight[pl.ds(start, half), :]
            rows_buf[c, group] = spread.astype(BF16).reshape(4, line, rows, WIDTH)
            if side == 0:
                sib_in[c] = send(rows_buf.at[c, group], from_sib.at[c], back_send.at[c, 0], back_recv.at[c, 0], sib)

    def add(c, group, value):
        rows_buf[c, k, group] = (rows_buf[c, k, group].astype(F32) + value.astype(F32)).astype(BF16)

    def stage_first(c):
        sib_in[c].wait_recv()
        one = 1 + c % 2
        for j in (one, 3, 3 - one, 0):
            add(c, secs[j], from_sib[c, secs[j]])
            if j == one:
                a = send(rows_buf.at[c, k, secs[one]], from_first.at[c, 0], back_send.at[c, 1], back_recv.at[c, 1], across[one])
            if j == 3:
                b = send(rows_buf.at[c, k, secs[3]], from_first.at[c, 1], back_send.at[c, 2], back_recv.at[c, 2], across[one])
        first_in[c] = [a, b]

    def stage_second(c):
        two = 2 - c % 2
        for copy in first_in[c]:
            copy.wait_recv()
        add(c, secs[two], from_first[c, 1])
        second_in[c] = send(rows_buf.at[c, k, secs[two]], from_second.at[c], back_send.at[c, 3], back_recv.at[c, 3], across[two])
        add(c, s, from_first[c, 0])

    def stage_line(c):
        second_in[c].wait_recv()
        add(c, s, from_second[c])
        line_in[c] = [
            send(
                rows_buf.at[c, k, s, lax.rem(m + j, line)], from_line.at[c, j - 1],
                back_line_send.at[c, j - 1], back_line_recv.at[c, j - 1], on_line(j),
            )
            for j in range(1, line)
        ]

    def stage_out(c):
        total = rows_buf[c, k, s, m].astype(F32)
        for j, copy in enumerate(line_in[c]):
            copy.wait_recv()
            total = total + from_line[c, j].astype(F32)
        out_ref[:, c * WIDTH : (c + 1) * WIDTH] = total.astype(BF16)

    schedule = ((0, stage_down), (1, stage_first), (3, stage_second), (5, stage_line), (7, stage_out))
    for i in range(chunks + 7):
        for lag, stage in schedule:
            if 0 <= i - lag < chunks:
                stage(i - lag)
    for copy in started:
        copy.wait_send()


def per_device(
    hidden,
    expert_ids,
    route_weights,
    w_gate_up,
    w_down,
    query_latent,
    query_rope,
    latent_cache,
    rope_cache,
    cache_lengths,
):
    rows, model_width = hidden.shape
    top_count = expert_ids.shape[1]
    members = lax.axis_size("dev")
    experts = lax.axis_size("sec") * members
    line = members // 2
    capacity = 2 * rows * top_count // experts
    slots = experts * capacity
    tokens = experts * rows
    units = w_down.shape[1]
    lanes = -(-experts // 128) * 128
    chunks = model_width // WIDTH
    pieces = chunks + 1
    att_rows = query_latent.shape[0]
    vmem = pl.BlockSpec(memory_space=pltpu.VMEM)
    smem = pl.BlockSpec(memory_space=pltpu.SMEM)
    hbm = pl.BlockSpec(memory_space=pl.ANY)
    dma = pltpu.SemaphoreType.DMA
    moe_out, load, attention_out = pl.pallas_call(
        functools.partial(kernel, (capacity, top_count)),
        out_shape=(
            jax.ShapeDtypeStruct((rows, model_width), BF16),
            jax.ShapeDtypeStruct((1, experts), F32),
            jax.ShapeDtypeStruct(query_latent.shape, BF16),
        ),
        in_specs=[vmem, vmem, vmem, smem, hbm, hbm, hbm, hbm, hbm, hbm],
        out_specs=(vmem, vmem, vmem),
        scratch_shapes=[
            pltpu.VMEM((chunks, 2, 4, line, rows, WIDTH), BF16),
            pltpu.VMEM((2, 4, line, rows, lanes), F32),
            pltpu.VMEM(w_gate_up.shape[1:], BF16),
            pltpu.VMEM(w_down.shape[1:], BF16),
            pltpu.VMEM(query_latent.shape, BF16),
            pltpu.VMEM(query_rope.shape, BF16),
            pltpu.VMEM(latent_cache.shape, BF16),
            pltpu.VMEM(rope_cache.shape, BF16),
            pltpu.VMEM((slots, 2 * units), F32),
            pltpu.VMEM((slots, units), BF16),
            pltpu.VMEM((slots, tokens), BF16),
            pltpu.VMEM((tokens, slots), BF16),
            pltpu.VMEM((tokens, 1), F32),
            pltpu.VMEM((chunks, 4, line, rows, WIDTH), BF16),
            pltpu.VMEM((chunks, 2, line, rows, WIDTH), BF16),
            pltpu.VMEM((chunks, line, rows, WIDTH), BF16),
            pltpu.VMEM((chunks, line - 1, rows, WIDTH), BF16),
            dma((chunks + 5,)),
            dma((pieces, line - 1)),
            dma((pieces, line - 1)),
            dma((pieces, 7)),
            dma((pieces, 7)),
            dma((chunks, 4)),
            dma((chunks, 4)),
            dma((chunks, line - 1)),
            dma((chunks, line - 1)),
        ],
        compiler_params=pltpu.CompilerParams(
            collective_id=0, has_side_effects=True, vmem_limit_bytes=62 * 1024 * 1024
        ),
        name="experts_and_attention",
    )(
        hidden, expert_ids.T, route_weights.T, cache_lengths, w_gate_up, w_down,
        query_latent, query_rope, latent_cache, rope_cache,
    )
    return (moe_out, load.reshape(experts), attention_out)


def solution(mesh):
    return jax.shard_map(
        per_device,
        mesh=mesh,
        in_specs=(
            P(("sec", "dev"), None),
            P(("sec", "dev"), None),
            P(("sec", "dev"), None),
            P(("sec", "dev"), None, None),
            P(("sec", "dev"), None, None),
            P(("sec", "dev"), None, None),
            P(("sec", "dev"), None, None),
            P(("sec", "dev"), None, None),
            P(("sec", "dev"), None, None),
            P(("sec", "dev")),
        ),
        out_specs=(P(("sec", "dev"), None), P(), P(("sec", "dev"), None, None)),
        check_vma=False,
    )
```

```python
import functools

import jax
import jax.numpy as jnp
from jax import lax
from jax.experimental import pallas as pl
from jax.experimental.pallas import tpu as pltpu
from jax.sharding import PartitionSpec as P

WIDTH = 512
MESH = pl.DeviceIdType.MESH
F32 = jnp.float32
BF16 = jnp.bfloat16


def kernel(
    slots_per,
    x_ref,
    ids_ref,
    route_ref,
    lengths_ref,
    gate_up_hbm,
    down_hbm,
    ql_hbm,
    qr_hbm,
    lat_hbm,
    rope_hbm,
    out_ref,
    load_ref,
    att_ref,
    rows_buf,
    table_buf,
    gate_up,
    down,
    ql,
    qr,
    lat,
    rope,
    projected,
    activated,
    placer,
    placer_t,
    weight,
    from_sib,
    from_first,
    from_second,
    from_line,
    local_sem,
    line_send,
    line_recv,
    hop_send,
    hop_recv,
    back_send,
    back_recv,
    back_line_send,
    back_line_recv,
):
    chunks = rows_buf.shape[0]
    line = rows_buf.shape[3]
    rows = x_ref.shape[0]
    tokens = 2 * 4 * line * rows
    units = down.shape[0]
    s = lax.axis_index("sec")
    d = lax.axis_index("dev")
    m = d // 2
    k = lax.rem(d, 2)
    experts = 8 * line
    me = s * (2 * line) + d

    def xor(j):
        low = lax.rem(s, 2)
        high = s // 2
        if j & 1:
            low = 1 - low
        if j & 2:
            high = 1 - high
        return high * 2 + low

    secs = [s, xor(1), xor(2), xor(3)]
    sib = (s, m * 2 + (1 - k))
    across = {1: (secs[1], d), 2: (secs[2], d)}

    def on_line(step):
        return (s, lax.rem(m + step, line) * 2 + k)

    local = []

    def fetch(src, dst):
        copy = pltpu.make_async_copy(src, dst, local_sem.at[len(local)])
        copy.start()
        local.append(copy)
        return copy

    partners = [sib, across[1], across[2]] + [on_line(i) for i in range(1, line)]
    barrier = pltpu.get_barrier_semaphore()
    for partner in partners:
        pl.semaphore_signal(barrier, inc=1, device_id=partner, device_id_type=MESH)
    att_copies = [fetch(a, b) for a, b in ((ql_hbm, ql), (qr_hbm, qr), (lat_hbm, lat), (rope_hbm, rope))]
    gate_copies = []

    def fetch_gate():
        cut = pl.ds(len(gate_copies) * WIDTH, WIDTH)
        gate_copies.append(fetch(gate_up_hbm.at[0, cut], gate_up.at[cut]))

    for _ in range(2):
        fetch_gate()
    lanes = table_buf.shape[-1]
    names = lax.broadcasted_iota(jnp.int32, (lanes, rows), 0)
    table = jnp.zeros((lanes, rows), F32)
    for j in range(ids_ref.shape[0]):
        table = table + jnp.where(names == ids_ref[j : j + 1, :], route_ref[j : j + 1, :], 0.0)
    table_buf[k, s, m] = table.T
    for c in range(chunks):
        rows_buf[c, k, s, m] = x_ref[:, c * WIDTH : (c + 1) * WIDTH]
    pl.semaphore_wait(barrier, len(partners))

    started = []

    def send(src, dst, send_sem, recv_sem, device):
        copy = pltpu.make_async_remote_copy(
            src_ref=src, dst_ref=dst, send_sem=send_sem, recv_sem=recv_sem,
            device_id=device, device_id_type=MESH,
        )
        copy.start()
        started.append(copy)
        return copy

    pieces = [table_buf] + [rows_buf.at[c] for c in range(chunks)]
    line_copies, own, fwd, sibs = {}, {}, {}, {}

    def stage_start(i):
        buf = pieces[i]
        line_copies[i] = [
            send(buf.at[k, s, m], buf.at[k, s, m], line_send.at[i, j - 1], line_recv.at[i, j - 1], on_line(j))
            for j in range(1, line)
        ]

    def hop(i, group, kind, device):
        buf = pieces[i]
        return send(buf.at[k, group], buf.at[k, group], hop_send.at[i, kind], hop_recv.at[i, kind], device)

    def stage_own(i):
        for copy in line_copies[i]:
            copy.wait_recv()
        own[i] = [hop(i, s, 0, across[1]), hop(i, s, 1, across[2])]

    def stage_cross(i):
        own[i][i % 2].wait_recv()
        fwd[i] = hop(i, secs[1 + i % 2], 2, across[2 - i % 2])
        own[i][1 - i % 2].wait_recv()

    def stage_diagonal(i):
        fwd[i].wait_recv()
        buf = pieces[i]
        sibs[i] = send(buf.at[k], buf.at[k], hop_send.at[i, 3], hop_recv.at[i, 3], sib)

    def routing():
        part = 8 * rows
        table = table_buf[...].reshape(tokens, lanes)
        chosen = (table > 0.0).astype(F32)
        load = jnp.sum(chosen, axis=0, keepdims=True) / float(tokens * slots_per[1] // experts)
        load_ref[...] = load[:, :experts]
        lane = lax.broadcasted_iota(jnp.int32, (tokens, lanes), 1)
        mine = jnp.sum(jnp.where(lane == me, table, 0.0), axis=1, keepdims=True)
        weight[...] = mine
        r = lax.broadcasted_iota(jnp.int32, (part, part), 0)
        q = lax.broadcasted_iota(jnp.int32, (part, part), 1)
        before = jnp.where((r // rows == q // rows) & (q < r), 1.0, 0.0).astype(BF16)
        for b in range(tokens // part):
            cut = slice(b * part, (b + 1) * part)
            hit = (mine[cut] > 0.0).astype(F32)
            rank = jnp.dot(before, jnp.broadcast_to(hit, (part, 128)).astype(BF16), preferred_element_type=F32)[:, :1]
            block = lax.broadcasted_iota(jnp.int32, (part, 1), 0) // rows + b * 8
            slot = jnp.where(hit > 0.0, block.astype(F32) * float(slots_per[0]) + rank, -1.0)
            spots = lax.broadcasted_iota(jnp.int32, (part, experts * slots_per[0]), 1).astype(F32)
            picks = jnp.where(spots == slot, 1.0, 0.0)
            placer_t[cut, :] = picks.astype(BF16)
            placer[:, cut] = picks.T.astype(BF16)

    def attend(r):
        scores = lax.dot_general(ql[r], lat[r], (((1,), (1,)), ((), ())), preferred_element_type=F32)
        scores = scores + lax.dot_general(qr[r], rope[r], (((0,), (0,)), ((), ())), preferred_element_type=F32)
        scores = scores * ((ql.shape[2] + qr.shape[1]) ** -0.5)
        positions = lax.broadcasted_iota(jnp.int32, scores.shape, 1)
        scores = jnp.where(positions < lengths_ref[r], scores, -1e30)
        powers = jnp.exp(scores - jnp.max(scores, axis=-1, keepdims=True))
        weights = (powers / jnp.sum(powers, axis=-1, keepdims=True)).astype(BF16)
        att_ref[r] = jnp.dot(weights, lat[r], preferred_element_type=F32).astype(BF16)

    def stage_up(i):
        sibs[i].wait_recv()
        if i == 0:
            routing()
            return
        c = i - 1
        gate_copies[c].wait()
        received = jnp.dot(
            placer[...], rows_buf[c].reshape(tokens, WIDTH), preferred_element_type=F32
        ).astype(BF16)

        @pl.loop(0, 2 * units // 512)
        def _(t):
            cols = pl.ds(pl.multiple_of(t * 512, 512), 512)
            part = jnp.dot(received, gate_up[pl.ds(c * WIDTH, WIDTH), cols], preferred_element_type=F32)
            if c == 0:
                projected[:, cols] = part
            else:
                projected[:, cols] += part

    count = chunks + 1
    for i in range(3):
        stage_start(i)
    for copy in att_copies:
        copy.wait()
    att_rows = ql.shape[0]
    attended = 0
    for i in range(count + 4):
        if i < count:
            if i + 3 < count:
                stage_start(i + 3)
            stage_own(i)
        if 0 <= i - 1 < count:
            stage_cross(i - 1)
        if 0 <= i - 3 < count:
            stage_diagonal(i - 3)
        if len(gate_copies) < chunks:
            fetch_gate()
        if i == 4:
            down_copy = fetch(down_hbm.at[0], down)
        if attended < att_rows and i >= 1:
            attend(attended)
            attended += 1
        if 0 <= i - 4 < count:
            stage_up(i - 4)
    for r in range(attended, att_rows):
        attend(r)
    for copy in started:
        copy.wait_send()

    for t in range(0, units, 256):
        gate = projected[:, t : t + 256]
        up = projected[:, units + t : units + t + 256]
        activated[:, t : t + 256] = (gate / (1.0 + jnp.exp(-gate)) * up).astype(BF16)
    down_copy.wait()

    started.clear()
    sib_in, first_in, second_in, line_in = {}, {}, {}, {}

    def stage_down(c):
        produced = jnp.dot(
            activated[...], down[:, c * WIDTH : (c + 1) * WIDTH], preferred_element_type=F32
        ).astype(BF16)
        half = tokens // 2
        for side in (0, 1):
            group = (1 - k) if side == 0 else k
            start = pl.multiple_of(group * half, half)
            spread = jnp.dot(placer_t[pl.ds(start, half), :], produced, preferred_element_type=F32)
            spread = spread * weight[pl.ds(start, half), :]
            rows_buf[c, group] = spread.astype(BF16).reshape(4, line, rows, WIDTH)
            if side == 0:
                sib_in[c] = send(rows_buf.at[c, group], from_sib.at[c], back_send.at[c, 0], back_recv.at[c, 0], sib)

    def add(c, group, value):
        rows_buf[c, k, group] = (rows_buf[c, k, group].astype(F32) + value.astype(F32)).astype(BF16)

    def stage_first(c):
        sib_in[c].wait_recv()
        one = 1 + c % 2
        for j in (one, 3, 3 - one, 0):
            add(c, secs[j], from_sib[c, secs[j]])
            if j == one:
                a = send(rows_buf.at[c, k, secs[one]], from_first.at[c, 0], back_send.at[c, 1], back_recv.at[c, 1], across[one])
            if j == 3:
                b = send(rows_buf.at[c, k, secs[3]], from_first.at[c, 1], back_send.at[c, 2], back_recv.at[c, 2], across[one])
        first_in[c] = [a, b]

    def stage_second(c):
        two = 2 - c % 2
        for copy in first_in[c]:
            copy.wait_recv()
        add(c, secs[two], from_first[c, 1])
        second_in[c] = send(rows_buf.at[c, k, secs[two]], from_second.at[c], back_send.at[c, 3], back_recv.at[c, 3], across[two])
        add(c, s, from_first[c, 0])

    def stage_line(c):
        second_in[c].wait_recv()
        add(c, s, from_second[c])
        line_in[c] = [
            send(
                rows_buf.at[c, k, s, lax.rem(m + j, line)], from_line.at[c, j - 1],
                back_line_send.at[c, j - 1], back_line_recv.at[c, j - 1], on_line(j),
            )
            for j in range(1, line)
        ]

    def stage_out(c):
        total = rows_buf[c, k, s, m].astype(F32)
        for j, copy in enumerate(line_in[c]):
            copy.wait_recv()
            total = total + from_line[c, j].astype(F32)
        out_ref[:, c * WIDTH : (c + 1) * WIDTH] = total.astype(BF16)

    schedule = ((0, stage_down), (1, stage_first), (3, stage_second), (5, stage_line), (7, stage_out))
    for i in range(chunks + 7):
        for lag, stage in schedule:
            if 0 <= i - lag < chunks:
                stage(i - lag)
    for copy in started:
        copy.wait_send()


def per_device(
    hidden,
    expert_ids,
    route_weights,
    w_gate_up,
    w_down,
    query_latent,
    query_rope,
    latent_cache,
    rope_cache,
    cache_lengths,
):
    rows, model_width = hidden.shape
    top_count = expert_ids.shape[1]
    members = lax.axis_size("dev")
    experts = lax.axis_size("sec") * members
    line = members // 2
    capacity = 2 * rows * top_count // experts
    slots = experts * capacity
    tokens = experts * rows
    units = w_down.shape[1]
    lanes = -(-experts // 128) * 128
    chunks = model_width // WIDTH
    pieces = chunks + 1
    att_rows = query_latent.shape[0]
    vmem = pl.BlockSpec(memory_space=pltpu.VMEM)
    smem = pl.BlockSpec(memory_space=pltpu.SMEM)
    hbm = pl.BlockSpec(memory_space=pl.ANY)
    dma = pltpu.SemaphoreType.DMA
    moe_out, load, attention_out = pl.pallas_call(
        functools.partial(kernel, (capacity, top_count)),
        out_shape=(
            jax.ShapeDtypeStruct((rows, model_width), BF16),
            jax.ShapeDtypeStruct((1, experts), F32),
            jax.ShapeDtypeStruct(query_latent.shape, BF16),
        ),
        in_specs=[vmem, vmem, vmem, smem, hbm, hbm, hbm, hbm, hbm, hbm],
        out_specs=(vmem, vmem, vmem),
        scratch_shapes=[
            pltpu.VMEM((chunks, 2, 4, line, rows, WIDTH), BF16),
            pltpu.VMEM((2, 4, line, rows, lanes), F32),
            pltpu.VMEM(w_gate_up.shape[1:], BF16),
            pltpu.VMEM(w_down.shape[1:], BF16),
            pltpu.VMEM(query_latent.shape, BF16),
            pltpu.VMEM(query_rope.shape, BF16),
            pltpu.VMEM(latent_cache.shape, BF16),
            pltpu.VMEM(rope_cache.shape, BF16),
            pltpu.VMEM((slots, 2 * units), F32),
            pltpu.VMEM((slots, units), BF16),
            pltpu.VMEM((slots, tokens), BF16),
            pltpu.VMEM((tokens, slots), BF16),
            pltpu.VMEM((tokens, 1), F32),
            pltpu.VMEM((chunks, 4, line, rows, WIDTH), BF16),
            pltpu.VMEM((chunks, 2, line, rows, WIDTH), BF16),
            pltpu.VMEM((chunks, line, rows, WIDTH), BF16),
            pltpu.VMEM((chunks, line - 1, rows, WIDTH), BF16),
            dma((chunks + 5,)),
            dma((pieces, line - 1)),
            dma((pieces, line - 1)),
            dma((pieces, 4)),
            dma((pieces, 4)),
            dma((chunks, 4)),
            dma((chunks, 4)),
            dma((chunks, line - 1)),
            dma((chunks, line - 1)),
        ],
        compiler_params=pltpu.CompilerParams(
            collective_id=0, has_side_effects=True, vmem_limit_bytes=62 * 1024 * 1024
        ),
        name="experts_and_attention",
    )(
        hidden, expert_ids.T, route_weights.T, cache_lengths, w_gate_up, w_down,
        query_latent, query_rope, latent_cache, rope_cache,
    )
    return (moe_out, load.reshape(experts), attention_out)


def solution(mesh):
    return jax.shard_map(
        per_device,
        mesh=mesh,
        in_specs=(
            P(("sec", "dev"), None),
            P(("sec", "dev"), None),
            P(("sec", "dev"), None),
            P(("sec", "dev"), None, None),
            P(("sec", "dev"), None, None),
            P(("sec", "dev"), None, None),
            P(("sec", "dev"), None, None),
            P(("sec", "dev"), None, None),
            P(("sec", "dev"), None, None),
            P(("sec", "dev")),
        ),
        out_specs=(P(("sec", "dev"), None), P(), P(("sec", "dev"), None, None)),
        check_vma=False,
    )
```
